32 devices in a mesh: row: 4 (over x, core), col: 8 (over z, y).
Axes of the slice: x: 2, y: 2, z: 4, core: 2. Of those that a mesh axis runs over, the one named last changes fastest.
Arguments:
- amplitudes: float32 [262144, 1024], P(('row', 'col')), may hold values from -6 to 6
- integrals: float32 [262144, 1024], P(('row', 'col')), may hold values from -0.0234375 to 0.0234375
- denominators: float32 [1024, 1024], P('col', 'row'), may hold values from 1 to 4
- history: float32 [8, 1024, 1024], P(None, 'col', 'row'), may hold values from -80 to 80
Outputs:
- extrapolated: float32 [1024, 1024], P('col', 'row')
- coefficients: float32 [8], replicated
The draws below stay inside these ranges and needn't reach their ends.
All inputs are finite; a program needn't handle non-finite values.
Results may differ from the reference program's by a relative error of at most 0.00005.
Values sent between devices are 32-bit elements; how exact they have to be, the bound alone decides.
A program may use at most 128 MiB of HBM per device.

```python
import jax
import jax.numpy as jnp
from jax import lax

OCC = 32
VBLK = 32
HIST = 8
CD = 262144
IJ = 1024
AB = 1024


def draw_history(key, part):
    keys = jax.random.split(jax.random.fold_in(key, 7), 1)
    base = jnp.clip(jax.random.normal(keys[0], (HIST, OCC * OCC, VBLK * VBLK), jnp.float32), -5.0, 5.0)
    pair_ij = jnp.arange(OCC * OCC, dtype=jnp.float32)[:, None] / (OCC * OCC)
    pair_ab = jnp.arange(VBLK * VBLK, dtype=jnp.float32)[None, :] / (VBLK * VBLK)
    ramp = 3.0 ** (0.5 * pair_ij + 0.5 * pair_ab)
    return base * ramp


def raised(entries, own_key, source, target, shards_of, factor):
    def block_of(axis_at):
        return (jnp.arange(entries.shape[axis_at]) // (entries.shape[axis_at] // shards_of)).reshape((-1,) + (1,) * (entries.ndim - 1 - axis_at))

    one_side = jax.random.permutation(own_key, shards_of)[block_of(target)]
    second = (block_of(target) + shards_of // 2) % shards_of
    return jnp.where((block_of(source) == one_side) | (block_of(source) == second), factor * entries, entries)


def shard_levels(rng, dims, pieces, least, high):
    loudness, own = 1.0, jax.random.fold_in(rng, 6)
    for axis_at, blocks in pieces:
        draws = jnp.exp(jax.random.uniform(jax.random.fold_in(own, axis_at), (blocks,), jnp.float32, least / len(pieces), high / len(pieces)))
        loudness = loudness * jnp.repeat(draws, dims[axis_at] // blocks).reshape([-1 if axis == axis_at else 1 for axis in range(len(dims))])
    return loudness


def noise(rng, extent, spread, limit, cuts=(), held_as=jnp.bfloat16):
    array = spread * jax.random.normal(rng, extent, jnp.float32)
    if cuts:
        array = array * shard_levels(rng, extent, cuts, -0.22, 0.18)
    return jnp.clip(array, -limit, limit).astype(held_as)


def bell_draw_with(rng, dims, width, bound, shards, heavy, kind=jnp.bfloat16):
    array = width * jax.random.normal(rng, dims, jnp.float32)
    if shards:
        array = array * shard_levels(rng, dims, shards, -0.22, 0.18)
    return jnp.clip(raised(array, jax.random.fold_in(rng, 3), *heavy), -bound, bound).astype(kind)


def setup_inputs(seed: int = 0) -> dict:
    arg_keys = jax.random.split(jax.random.key(seed), 5)
    amplitudes = noise(arg_keys[0], (CD, IJ), 1.0, 6.0, ((0, 32),), jnp.float32)
    integrals = bell_draw_with(arg_keys[1], (CD, AB), CD ** -0.5, 0.0234375, ((0, 32),), (0, 1, 32, 2.75), jnp.float32)
    denominators = jnp.clip(1.0 + 3.0 * jax.random.uniform(arg_keys[2], (IJ, AB), jnp.float32) ** shard_levels(arg_keys[2], (IJ, AB), ((0, 8), (1, 4)), -0.2, 0.2), 1.0, 4.0)
    history = draw_history(jax.random.fold_in(arg_keys[4], 71), 0)
    return {"amplitudes": amplitudes, "integrals": integrals, "denominators": denominators, "history": history}


def flip(field):
    return field.reshape(OCC, OCC, VBLK, VBLK).transpose(1, 0, 3, 2).reshape(OCC * OCC, VBLK * VBLK)

def weights_of(gram):
    count = gram.shape[0]
    ridge = 1e-06 * jnp.trace(gram) / count
    factor = jnp.linalg.cholesky(gram + ridge * jnp.eye(count, dtype=gram.dtype))
    ones = jnp.ones((count, 1), gram.dtype)
    half = lax.linalg.triangular_solve(factor, ones, left_side=True, lower=True)
    whole = lax.linalg.triangular_solve(factor, half, left_side=True, lower=True, transpose_a=True)
    return whole[:, 0] / jnp.sum(whole)

def reference(amplitudes, integrals, denominators, history):
    ladder = lax.dot_general(amplitudes.astype(jnp.float32), integrals.astype(jnp.float32), (((0,), (0,)), ((), ())), precision=lax.Precision.HIGHEST, preferred_element_type=jnp.float32)
    symmetric = ladder + flip(ladder)
    update = symmetric / denominators
    following = jnp.concatenate([history[1:], update[None]], axis=0)
    errors = following - history
    gram = jnp.einsum('kxy,lxy->kl', errors, errors, precision=lax.Precision.HIGHEST)
    coefficients = weights_of(gram)
    extrapolated = jnp.einsum('k,kxy->xy', coefficients, following, precision=lax.Precision.HIGHEST)
    return (extrapolated, coefficients)
```

```python
import functools

import jax
import jax.numpy as jnp
from jax import lax
from jax.experimental import pallas as pl
from jax.experimental.pallas import tpu as pltpu
from jax.sharding import PartitionSpec as P

OCC = 32
VBLK = 32
MESH = pl.DeviceIdType.MESH
F32 = jnp.float32
BF16 = jnp.bfloat16
SLOTS = 3
MIB = 1 << 20


def ring_place(row, n_row):
    return jnp.where(lax.rem(row, 2) == 0, row // 2, n_row - 1 - row // 2)


def ring_row(place, n_row):
    return jnp.where(place < n_row // 2, 2 * place, 2 * (n_row - 1 - place) + 1)


def two_parts(x):
    high = x.astype(BF16)
    return high, (x - high.astype(F32)).astype(BF16)


def dot(a, b):
    return jnp.dot(a, b, preferred_element_type=F32)


def ladder_kernel(
    n_row, n_col, n_sub, kb,
    t_hbm, v_hbm, out_ref,
    t_high, t_low, v_high, v_low, t_stage, v_stage, first, ring, pair, line,
    t_sem, v_sem, ring_send, ring_recv, pair_send, pair_recv, line_send, line_recv,
):
    depth, pairs = t_hbm.shape
    width = v_hbm.shape[1] // n_row
    rows = pairs // n_col
    q = rows // n_sub
    sub = n_col * q
    half = sub // 2
    n_line = n_col // 2
    blocks = depth // kb
    per_sub = blocks // n_sub
    kc = kb * n_sub
    row = lax.axis_index("row")
    col = lax.axis_index("col")
    place = ring_place(row, n_row)
    after = ring_row(lax.rem(place + 1, n_row), n_row)
    before = ring_row(lax.rem(place + n_row - 1, n_row), n_row)
    side = lax.rem(col, 2)
    along = col // 2
    other = along * 2 + 1 - side

    def line_col(k):
        return lax.rem(along + k, n_line) * 2 + side

    barrier = pltpu.get_barrier_semaphore()
    peers = [(after, col), (before, col), (row, other)]
    peers += [(row, line_col(k)) for k in range(1, n_line)]
    for peer in peers:
        pl.semaphore_signal(barrier, inc=1, device_id=peer, device_id_type=MESH)

    def columns(step):
        owner = ring_row(lax.rem(place - 1 - step + 2 * n_row, n_row), n_row)
        return pl.ds(pl.multiple_of(owner * width, width), width)

    def t_copy(b):
        slot = lax.rem(b, SLOTS)
        at = pl.multiple_of(b * kb, kb)
        return pltpu.make_async_copy(t_hbm.at[pl.ds(at, kb), :], t_stage.at[slot], t_sem.at[slot])

    def v_copy(step, b):
        slot = lax.rem(b, SLOTS)
        at = pl.multiple_of(b * kb, kb)
        return pltpu.make_async_copy(
            v_hbm.at[pl.ds(at, kb), columns(step)],
            v_stage.at[step % 2, slot],
            v_sem.at[step % 2, slot],
        )

    def keep_v(step, b):
        at = pl.multiple_of(b * kb, kb)
        high, low = two_parts(v_stage[step % 2, lax.rem(b, SLOTS)])
        v_high[step % 2, pl.ds(at, kb), :] = high
        v_low[step % 2, pl.ds(at, kb), :] = low
        return high, low

    def ring_copy(step, m):
        source = first if step == 0 else ring.at[step - 1]
        return pltpu.make_async_remote_copy(
            source.at[m], ring.at[step, m],
            ring_send.at[step, m], ring_recv.at[step, m],
            device_id=(after, col), device_id_type=MESH,
        )

    def pair_copy(m):
        at = pl.multiple_of((1 - side) * half, half)
        return pltpu.make_async_remote_copy(
            ring.at[n_row - 2, m, pl.ds(at, half), :], pair.at[m],
            pair_send.at[m], pair_recv.at[m],
            device_id=(row, other), device_id_type=MESH,
        )

    def line_copy(m, k):
        at = pl.multiple_of(lax.rem(along + k, n_line) * q, q)
        return pltpu.make_async_remote_copy(
            pair.at[m, pl.ds(at, q), :], line.at[m, k - 1],
            line_send.at[m, k - 1], line_recv.at[m, k - 1],
            device_id=(row, line_col(k)), device_id_type=MESH,
        )

    for b in range(SLOTS):
        t_copy(b).start()
        v_copy(0, b).start()
        v_copy(1, b).start()
    first[...] = jnp.zeros_like(first)

    def load(b, carry):
        t_copy(b).wait()
        v_copy(0, b).wait()
        v_copy(1, b).wait()
        at = pl.multiple_of(b * kb, kb)
        vh, vl = keep_v(0, b)
        keep_v(1, b)
        slot = lax.rem(b, SLOTS)
        for c in range(n_col):
            turned = t_stage[slot, :, c * rows:(c + 1) * rows].T
            th, tl = two_parts(turned)
            for m in range(n_sub):
                to = m * sub + ((c % 2) * n_line + c // 2) * q
                t_high[to:to + q, pl.ds(at, kb)] = th[m * q:(m + 1) * q]
                t_low[to:to + q, pl.ds(at, kb)] = tl[m * q:(m + 1) * q]

        @pl.when(b + SLOTS < blocks)
        def _():
            t_copy(b + SLOTS).start()
            v_copy(0, b + SLOTS).start()
            v_copy(1, b + SLOTS).start()

        for m in range(n_sub):
            th = t_high[m * sub:(m + 1) * sub, pl.ds(at, kb)]
            tl = t_low[m * sub:(m + 1) * sub, pl.ds(at, kb)]
            first[m] += dot(th, vh) + dot(th, vl) + dot(tl, vh)
        return carry

    lax.fori_loop(0, blocks, load, 0)

    pl.semaphore_wait(barrier, len(peers))
    for b in range(SLOTS):
        v_copy(2, b).start()
    for m in range(n_sub):
        ring_copy(0, m).start()

    def spread(m):
        pair_copy(m).wait_recv()
        at = pl.multiple_of(side * half, half)
        pair[m] += ring[n_row - 2, m, pl.ds(at, half), :]
        for k in range(1, n_line):
            line_copy(m, k).start()

    for step in range(1, n_row):
        if step + 2 < n_row:
            for b in range(SLOTS):
                v_copy(step + 2, b).start()
        for m in range(n_sub):
            first_rows = slice(m * sub, (m + 1) * sub)
            ring_copy(step - 1, m).wait_recv()

            def more(i, carry, step=step, m=m, first_rows=first_rows):
                if step < n_row - 1:
                    b = m * per_sub + i
                    v_copy(step + 1, b).wait()
                    keep_v(step + 1, b)

                    @pl.when(b + SLOTS < blocks)
                    def _():
                        v_copy(step + 1, b + SLOTS).start()

                at = pl.ds(pl.multiple_of(i * kc, kc), kc)
                th = t_high[first_rows, at]
                tl = t_low[first_rows, at]
                vh = v_high[step % 2, at, :]
                vl = v_low[step % 2, at, :]
                ring[step - 1, m] += dot(th, vh) + dot(th, vl) + dot(tl, vh)
                return carry

            lax.fori_loop(0, per_sub, more, 0)
            if step < n_row - 1:
                ring_copy(step, m).start()
            else:
                pair_copy(m).start()
                if m > 0:
                    spread(m - 1)
    spread(n_sub - 1)
    for m in range(n_sub):
        mine = pair[m, pl.ds(pl.multiple_of(along * q, q), q), :]
        for k in range(1, n_line):
            line_copy(m, k).wait_recv()
            mine += line[m, k - 1]
        out_ref[m * q:(m + 1) * q, :] = mine
    for m in range(n_sub):
        for step in range(n_row - 1):
            ring_copy(step, m).wait_send()
        pair_copy(m).wait_send()
        for k in range(1, n_line):
            line_copy(m, k).wait_send()


def ladder_block(amplitudes, integrals):
    n_col = lax.axis_size("col")
    n_row = lax.axis_size("row")
    depth, pairs = amplitudes.shape
    width = integrals.shape[1] // n_row
    rows = pairs // n_col
    n_sub = min(4, rows // 16)
    kb = min(256, depth // n_sub)
    q = rows // n_sub
    sub = n_col * q
    n_line = n_col // 2
    dma = pltpu.SemaphoreType.DMA
    return pl.pallas_call(
        functools.partial(ladder_kernel, n_row, n_col, n_sub, kb),
        out_shape=jax.ShapeDtypeStruct((rows, width), F32),
        in_specs=[pl.BlockSpec(memory_space=pl.ANY)] * 2,
        out_specs=pl.BlockSpec(memory_space=pltpu.VMEM),
        scratch_shapes=[
            pltpu.VMEM((pairs, depth), BF16),
            pltpu.VMEM((pairs, depth), BF16),
            pltpu.VMEM((2, depth, width), BF16),
            pltpu.VMEM((2, depth, width), BF16),
            pltpu.VMEM((SLOTS, kb, pairs), F32),
            pltpu.VMEM((2, SLOTS, kb, width), F32),
            pltpu.VMEM((n_sub, sub, width), F32),
            pltpu.VMEM((n_row - 1, n_sub, sub, width), F32),
            pltpu.VMEM((n_sub, sub // 2, width), F32),
            pltpu.VMEM((n_sub, n_line - 1, q, width), F32),
            dma((SLOTS,)),
            dma((2, SLOTS)),
            dma((n_row - 1, n_sub)),
            dma((n_row - 1, n_sub)),
            dma((n_sub,)),
            dma((n_sub,)),
            dma((n_sub, n_line - 1)),
            dma((n_sub, n_line - 1)),
        ],
        compiler_params=pltpu.CompilerParams(
            collective_id=0, has_side_effects=True, vmem_limit_bytes=60 * MIB
        ),
        cost_estimate=pl.CostEstimate(
            flops=6 * depth * pairs * pairs, bytes_accessed=8 * depth * pairs, transcendentals=0
        ),
    )(amplitudes, integrals)


def weights_of(gram):
    count = gram.shape[0]
    ridge = 1e-06 * jnp.trace(gram) / count
    factor = jnp.linalg.cholesky(gram + ridge * jnp.eye(count, dtype=gram.dtype))
    ones = jnp.ones((count, 1), gram.dtype)
    half = lax.linalg.triangular_solve(factor, ones, left_side=True, lower=True)
    whole = lax.linalg.triangular_solve(factor, half, left_side=True, lower=True, transpose_a=True)
    return whole[:, 0] / jnp.sum(whole)


def shards(amplitudes, integrals, denominators, history):
    n_col = lax.axis_size("col")
    n_row = lax.axis_size("row")
    occ_group = OCC // n_col
    vir_group = VBLK // n_row
    block = ladder_block(amplitudes, integrals)
    shaped = block.reshape(occ_group, n_col, occ_group, vir_group, n_row, vir_group)
    swapped = lax.all_to_all(
        lax.all_to_all(shaped, "row", split_axis=4, concat_axis=4, tiled=True),
        "col",
        split_axis=1,
        concat_axis=1,
        tiled=True,
    )
    mirror_part = swapped.transpose(2, 1, 0, 5, 4, 3).reshape(block.shape)
    symmetric = block + mirror_part
    update = symmetric / denominators
    following = jnp.concatenate([history[1:], update[None]], axis=0)
    errors = following - history
    gram = lax.psum(
        jnp.einsum("kxy,lxy->kl", errors, errors, precision=lax.Precision.HIGHEST), ("row", "col")
    )
    coefficients = weights_of(gram)
    extrapolated = jnp.einsum("k,kxy->xy", coefficients, following, precision=lax.Precision.HIGHEST)
    return (extrapolated, coefficients)


def solution(mesh):
    return jax.shard_map(
        shards,
        mesh=mesh,
        in_specs=(
            P(("row", "col"), None),
            P(("row", "col"), None),
            P("col", "row"),
            P(None, "col", "row"),
        ),
        out_specs=(P("col", "row"), P()),
        check_vma=False,
    )
```

```python
import functools

import jax
import jax.numpy as jnp
from jax import lax
from jax.experimental import pallas as pl
from jax.experimental.pallas import tpu as pltpu
from jax.sharding import PartitionSpec as P

OCC = 32
VBLK = 32
MESH = pl.DeviceIdType.MESH
F32 = jnp.float32
BF16 = jnp.bfloat16
SLOTS = 3
MIB = 1 << 20


def ring_place(row, n_row):
    return jnp.where(lax.rem(row, 2) == 0, row // 2, n_row - 1 - row // 2)


def ring_row(place, n_row):
    return jnp.where(place < n_row // 2, 2 * place, 2 * (n_row - 1 - place) + 1)


def two_parts(x):
    high = x.astype(BF16)
    return high, (x - high.astype(F32)).astype(BF16)


def dot(a, b):
    return jnp.dot(a, b, preferred_element_type=F32)


def ladder_kernel(
    n_row, n_col, n_sub, kb,
    t_hbm, v_hbm, out_ref,
    t_high, t_low, v_high, v_low, t_stage, v_stage, first, ring, pair, line,
    t_sem, v_sem, ring_send, ring_recv, pair_send, pair_recv, line_send, line_recv,
):
    depth, pairs = t_hbm.shape
    width = v_hbm.shape[1] // n_row
    rows = pairs // n_col
    q = rows // n_sub
    sub = n_col * q
    half = sub // 2
    n_line = n_col // 2
    blocks = depth // kb
    per_sub = blocks // n_sub
    kc = kb * n_sub
    row = lax.axis_index("row")
    col = lax.axis_index("col")
    place = ring_place(row, n_row)
    after = ring_row(lax.rem(place + 1, n_row), n_row)
    before = ring_row(lax.rem(place + n_row - 1, n_row), n_row)
    side = lax.rem(col, 2)
    along = col // 2
    other = along * 2 + 1 - side

    def line_col(k):
        return lax.rem(along + k, n_line) * 2 + side

    barrier = pltpu.get_barrier_semaphore()
    peers = [(after, col), (before, col), (row, other)]
    peers += [(row, line_col(k)) for k in range(1, n_line)]
    for peer in peers:
        pl.semaphore_signal(barrier, inc=1, device_id=peer, device_id_type=MESH)

    def columns(step):
        owner = ring_row(lax.rem(place - 1 - step + 2 * n_row, n_row), n_row)
        return pl.ds(pl.multiple_of(owner * width, width), width)

    def t_copy(b):
        slot = lax.rem(b, SLOTS)
        at = pl.multiple_of(b * kb, kb)
        return pltpu.make_async_copy(t_hbm.at[pl.ds(at, kb), :], t_stage.at[slot], t_sem.at[slot])

    def v_copy(step, b):
        slot = lax.rem(b, SLOTS)
        at = pl.multiple_of(b * kb, kb)
        return pltpu.make_async_copy(
            v_hbm.at[pl.ds(at, kb), columns(step)],
            v_stage.at[step % 2, slot],
            v_sem.at[step % 2, slot],
        )

    def keep_v(step, b):
        at = pl.multiple_of(b * kb, kb)
        high, low = two_parts(v_stage[step % 2, lax.rem(b, SLOTS)])
        v_high[step % 2, pl.ds(at, kb), :] = high
        v_low[step % 2, pl.ds(at, kb), :] = low
        return high, low

    def ring_copy(step, m):
        source = first if step == 0 else ring.at[step - 1]
        return pltpu.make_async_remote_copy(
            source.at[m], ring.at[step, m],
            ring_send.at[step, m], ring_recv.at[step, m],
            device_id=(after, col), device_id_type=MESH,
        )

    def pair_copy(m):
        at = pl.multiple_of((1 - side) * half, half)
        return pltpu.make_async_remote_copy(
            ring.at[n_row - 2, m, pl.ds(at, half), :], pair.at[m],
            pair_send.at[m], pair_recv.at[m],
            device_id=(row, other), device_id_type=MESH,
        )

    def line_copy(m, k):
        at = pl.multiple_of(lax.rem(along + k, n_line) * q, q)
        return pltpu.make_async_remote_copy(
            pair.at[m, pl.ds(at, q), :], line.at[m, k - 1],
            line_send.at[m, k - 1], line_recv.at[m, k - 1],
            device_id=(row, line_col(k)), device_id_type=MESH,
        )

    for b in range(SLOTS):
        t_copy(b).start()
        v_copy(0, b).start()
        v_copy(1, b).start()
    first[...] = jnp.zeros_like(first)

    def load(b, carry):
        t_copy(b).wait()
        v_copy(0, b).wait()
        v_copy(1, b).wait()
        at = pl.multiple_of(b * kb, kb)
        vh, vl = keep_v(0, b)
        keep_v(1, b)
        slot = lax.rem(b, SLOTS)
        for c in range(n_col):
            turned = t_stage[slot, :, c * rows:(c + 1) * rows].T
            th, tl = two_parts(turned)
            for m in range(n_sub):
                to = m * sub + ((c % 2) * n_line + c // 2) * q
                t_high[to:to + q, pl.ds(at, kb)] = th[m * q:(m + 1) * q]
                t_low[to:to + q, pl.ds(at, kb)] = tl[m * q:(m + 1) * q]

        @pl.when(b + SLOTS < blocks)
        def _():
            t_copy(b + SLOTS).start()
            v_copy(0, b + SLOTS).start()
            v_copy(1, b + SLOTS).start()

        for m in range(n_sub):
            th = t_high[m * sub:(m + 1) * sub, pl.ds(at, kb)]
            tl = t_low[m * sub:(m + 1) * sub, pl.ds(at, kb)]
            first[m] += dot(th, vh) + dot(th, vl) + dot(tl, vh)
        return carry

    lax.fori_loop(0, blocks, load, 0)

    pl.semaphore_wait(barrier, len(peers))
    for b in range(SLOTS):
        v_copy(2, b).start()
    for m in range(n_sub):
        ring_copy(0, m).start()

    def spread(m):
        pair_copy(m).wait_recv()
        at = pl.multiple_of(side * half, half)
        pair[m] += ring[n_row - 2, m, pl.ds(at, half), :]
        for k in range(1, n_line):
            line_copy(m, k).start()

    for step in range(1, n_row):
        if step + 2 < n_row:
            for b in range(SLOTS):
                v_copy(step + 2, b).start()
        for m in range(n_sub):
            first_rows = slice(m * sub, (m + 1) * sub)
            ring_copy(step - 1, m).wait_recv()

            def more(i, carry, step=step, m=m, first_rows=first_rows):
                if step < n_row - 1:
                    b = m * per_sub + i
                    v_copy(step + 1, b).wait()
                    keep_v(step + 1, b)

                    @pl.when(b + SLOTS < blocks)
                    def _():
                        v_copy(step + 1, b + SLOTS).start()

                at = pl.ds(pl.multiple_of(i * kc, kc), kc)
                th = t_high[first_rows, at]
                tl = t_low[first_rows, at]
                vh = v_high[step % 2, at, :]
                vl = v_low[step % 2, at, :]
                ring[step - 1, m] += dot(th, vh) + dot(th, vl) + dot(tl, vh)
                return carry

            lax.fori_loop(0, per_sub, more, 0)
            if step < n_row - 1:
                ring_copy(step, m).start()
            else:
                pair_copy(m).start()
                if m > 0:
                    spread(m - 1)
    spread(n_sub - 1)
    for m in range(n_sub):
        mine = pair[m, pl.ds(pl.multiple_of(along * q, q), q), :]
        for k in range(1, n_line):
            line_copy(m, k).wait_recv()
            mine += line[m, k - 1]
        out_ref[m * q:(m + 1) * q, :] = mine
    for m in range(n_sub):
        for step in range(n_row - 1):
            ring_copy(step, m).wait_send()
        pair_copy(m).wait_send()
        for k in range(1, n_line):
            line_copy(m, k).wait_send()


def ladder_block(amplitudes, integrals):
    n_col = lax.axis_size("col")
    n_row = lax.axis_size("row")
    depth, pairs = amplitudes.shape
    width = integrals.shape[1] // n_row
    rows = pairs // n_col
    n_sub = min(4, rows // 16)
    kb = min(256, depth // n_sub)
    q = rows // n_sub
    sub = n_col * q
    n_line = n_col // 2
    dma = pltpu.SemaphoreType.DMA
    return pl.pallas_call(
        functools.partial(ladder_kernel, n_row, n_col, n_sub, kb),
        out_shape=jax.ShapeDtypeStruct((rows, width), F32),
        in_specs=[pl.BlockSpec(memory_space=pl.ANY)] * 2,
        out_specs=pl.BlockSpec(memory_space=pltpu.VMEM),
        scratch_shapes=[
            pltpu.VMEM((pairs, depth), BF16),
            pltpu.VMEM((pairs, depth), BF16),
            pltpu.VMEM((2, depth, width), BF16),
            pltpu.VMEM((2, depth, width), BF16),
            pltpu.VMEM((SLOTS, kb, pairs), F32),
            pltpu.VMEM((2, SLOTS, kb, width), F32),
            pltpu.VMEM((n_sub, sub, width), F32),
            pltpu.VMEM((n_row - 1, n_sub, sub, width), F32),
            pltpu.VMEM((n_sub, sub // 2, width), F32),
            pltpu.VMEM((n_sub, n_line - 1, q, width), F32),
            dma((SLOTS,)),
            dma((2, SLOTS)),
            dma((n_row - 1, n_sub)),
            dma((n_row - 1, n_sub)),
            dma((n_sub,)),
            dma((n_sub,)),
            dma((n_sub, n_line - 1)),
            dma((n_sub, n_line - 1)),
        ],
        compiler_params=pltpu.CompilerParams(
            collective_id=0, has_side_effects=True, vmem_limit_bytes=60 * MIB
        ),
        cost_estimate=pl.CostEstimate(
            flops=6 * depth * pairs * pairs, bytes_accessed=8 * depth * pairs, transcendentals=0
        ),
    )(amplitudes, integrals)


def exact(a, b):
    return jnp.dot(a, b, precision=lax.Precision.HIGHEST, preferred_element_type=F32)


def finish_kernel(
    n_row, n_col, group, lanes,
    block_ref, den_ref, hist_ref, out_ref, coef_ref,
    packed, landed, grams, send_sem, recv_sem, gram_send, gram_recv,
):
    count = hist_ref.shape[0]
    rows, width = block_ref.shape
    og = OCC // n_col
    vg = VBLK // n_row
    n = n_row * n_col
    row = lax.axis_index("row")
    col = lax.axis_index("col")
    me = row * n_col + col

    def peer(k):
        to = lax.rem(me + k, n)
        return to // n_col, lax.rem(to, n_col)

    def spot(of_row, of_col):
        return (
            pl.ds(pl.multiple_of(of_col * group, group), group),
            pl.ds(pl.multiple_of(of_row * lanes, lanes), lanes),
        )

    def mirror_copy(k, target):
        to_row, to_col = peer(k)
        return pltpu.make_async_remote_copy(
            packed.at[spot(to_row, to_col)], landed.at[target],
            send_sem.at[k - 1], recv_sem.at[k - 1],
            device_id=(to_row, to_col), device_id_type=MESH,
        )

    def gram_copy(k, slot):
        return pltpu.make_async_remote_copy(
            grams.at[me], grams.at[slot],
            gram_send.at[k - 1], gram_recv.at[k - 1],
            device_id=peer(k), device_id_type=MESH,
        )

    def each(body):
        def step(k, carry):
            body(k)
            return carry

        lax.fori_loop(1, n, step, 0)

    barrier = pltpu.get_barrier_semaphore()
    each(lambda k: pl.semaphore_signal(barrier, inc=1, device_id=peer(k), device_id_type=MESH))

    def iota(shape, axis):
        return lax.broadcasted_iota(jnp.int32, shape, axis)

    def hot(hits):
        return jnp.where(hits, 1.0, 0.0).astype(F32)

    shape = (n_col * group, rows)
    at = iota(shape, 1)
    j = at % OCC
    take_rows = hot(iota(shape, 0) == (j // og) * group + (at // OCC) * og + j % og)
    shape = (width, n_row * lanes)
    at = iota(shape, 0)
    b = at % VBLK
    take_lanes = hot(iota(shape, 1) == (b // vg) * lanes + (at // VBLK) * vg + b % vg)
    packed[...] = exact(exact(take_rows, block_ref[...]), take_lanes)
    landed[spot(row, col)] = packed[spot(row, col)]

    pl.semaphore_wait(barrier, n - 1)
    each(lambda k: mirror_copy(k, spot(row, col)).start())

    shape = (rows, n_col * group)
    at = iota(shape, 0)
    i = at % OCC
    give_rows = hot(iota(shape, 1) == (i // og) * group + (i % og) * og + at // OCC)
    shape = (n_row * lanes, width)
    at = iota(shape, 1)
    a = at % VBLK
    give_lanes = hot(iota(shape, 0) == (a // vg) * lanes + (a % vg) * vg + at // VBLK)

    tile = (count, 128)
    down = iota(tile, 0)
    over = iota(tile, 1)

    def place(total, k, l, x, y):
        value = jnp.sum(jnp.sum(x * y, axis=0, keepdims=True), axis=1, keepdims=True)
        hits = ((down == k) & (over == l)) | ((down == l) & (over == k))
        return jnp.where(hits, value, total)

    def step_of(k):
        return hist_ref[k + 1] - hist_ref[k]

    gram = jnp.zeros(tile, F32)
    for k in range(count - 1):
        for l in range(k, count - 1):
            gram = place(gram, k, l, step_of(k), step_of(l))

    def arrive(k):
        source = lax.rem(me + n - k, n)
        mirror_copy(k, spot(source // n_col, lax.rem(source, n_col))).wait_recv()

    each(arrive)
    symmetric = block_ref[...] + exact(exact(give_rows, landed[...]), give_lanes)
    update = symmetric / den_ref[...]
    out_ref[...] = update
    last = update - hist_ref[count - 1]
    for k in range(count - 1):
        gram = place(gram, k, count - 1, step_of(k), last)
    gram = place(gram, count - 1, count - 1, last, last)
    grams[me] = gram
    each(lambda k: gram_copy(k, me).start())
    each(lambda k: gram_copy(k, lax.rem(me + n - k, n)).wait_recv())
    total = lax.fori_loop(0, n, lambda d, sofar: sofar + grams[d], jnp.zeros(tile, F32))

    diagonal = jnp.where(down == over, total, 0.0)
    trace = jnp.sum(jnp.sum(diagonal, axis=0, keepdims=True), axis=1, keepdims=True)
    ridge = 1e-06 * trace / count
    system = jnp.where(down == over, total + ridge, total)
    system = jnp.where(over == count, 1.0, system)
    for k in range(count):
        pivot = system[k:k + 1, :] / system[k:k + 1, k:k + 1]
        system = jnp.where(down == k, pivot, system - system[:, k:k + 1] * pivot)
    y = system[:, count:count + 1]
    weights = y / jnp.sum(y, axis=0, keepdims=True)
    coef_ref[...] = weights
    result = weights[count - 1:count, :] * out_ref[...]
    for k in range(count - 1):
        result += weights[k:k + 1, :] * hist_ref[k + 1]
    out_ref[...] = result
    each(lambda k: mirror_copy(k, spot(row, col)).wait_send())
    each(lambda k: gram_copy(k, me).wait_send())


def finish(block, denominators, history):
    n_col = lax.axis_size("col")
    n_row = lax.axis_size("row")
    n = n_row * n_col
    count = history.shape[0]
    group = -(-((OCC // n_col) ** 2) // 8) * 8
    lanes = -(-((VBLK // n_row) ** 2) // 128) * 128
    vmem = pl.BlockSpec(memory_space=pltpu.VMEM)
    dma = pltpu.SemaphoreType.DMA
    return pl.pallas_call(
        functools.partial(finish_kernel, n_row, n_col, group, lanes),
        out_shape=(
            jax.ShapeDtypeStruct(block.shape, F32),
            jax.ShapeDtypeStruct((count, 1), F32),
        ),
        in_specs=[vmem] * 3,
        out_specs=(vmem, vmem),
        scratch_shapes=[
            pltpu.VMEM((n_col * group, n_row * lanes), F32),
            pltpu.VMEM((n_col * group, n_row * lanes), F32),
            pltpu.VMEM((n, count, 128), F32),
            dma((n - 1,)),
            dma((n - 1,)),
            dma((n - 1,)),
            dma((n - 1,)),
        ],
        compiler_params=pltpu.CompilerParams(
            collective_id=1, has_side_effects=True, vmem_limit_bytes=32 * MIB
        ),
    )(block, denominators, history)


def shards(amplitudes, integrals, denominators, history):
    block = ladder_block(amplitudes, integrals)
    extrapolated, coefficients = finish(block, denominators, history)
    return (extrapolated, coefficients[:, 0])


def solution(mesh):
    return jax.shard_map(
        shards,
        mesh=mesh,
        in_specs=(
            P(("row", "col"), None),
            P(("row", "col"), None),
            P("col", "row"),
            P(None, "col", "row"),
        ),
        out_specs=(P("col", "row"), P()),
        check_vma=False,
    )
```
